1024 devices in a mesh: grp: 32 (over z, core), mem: 32 (over y, x).
Axes of the slice: x: 4, y: 8, z: 16, core: 2. Of those that a mesh axis runs over, the one named last changes fastest.
Arguments:
- t_store: bfloat16 [16384, 4, 4096], P(('grp', 'mem')), may hold values from -6 to 6
- v_blocks: bfloat16 [11264, 32, 4096], P(('grp', 'mem')), may hold values from -0.0048828125 to 0.0048828125
- block_id: int32 [32, 32], P('grp'), may hold values from 0 to 31, each once within a row
- tile_home: int32 [32, 512], P('grp'), may hold values from 0 to 511, as said below
- task_slab: int32 [32, 32, 11], P('grp'), may hold values from 0 to 31, as said below
Outputs:
- ladder: float32 [64, 1024], P('grp', 'mem')
The draws below stay inside these ranges and needn't reach their ends.
Inputs may be any that keep to these rules, and one draw needn't show every extreme that they name: `block_id`: each row is a permutation: every cd tile pair of a group is taken by exactly one mem device of it. tile_home[g, q*16+o] = m*16+s places occupied block o of cd tile pair q of group g in slot s of mem device m of that group; each row is a permutation; the tiles of one cd tile pair lie on cyclically consecutive mem devices, tile o on the device after that of tile o-1, so each mem device holds at most 1 tiles of every cd tile pair. The 11 entries of task_slab[g, d] are distinct ab slabs; slabs k*1 to k + 1 - 1 are the slabs of mem device k, and every device's entries include all 1 slabs of at least one mem device.
All inputs are finite; a program needn't handle non-finite values.
Results may differ from the reference program's by a relative error of at most 0.0003.
Values may be sent and summed in bfloat16 or wider, within the bound.
A program may use at most 32 MiB of HBM per device.

```python
import jax
import jax.numpy as jnp
from jax import lax

OT = 4
NOB = 16
VB = 11
SLABS = 32
N = 32
K = 4096
SLABS_PER_MEMORY = 1
N_GRP = 32
N_MEM = 32


def shuffled_starts(group_key):
    return jax.random.permutation(group_key, N_MEM).astype(jnp.int32)


def draw_tile_home(key, part):
    key = jax.random.fold_in(key, 11)
    group_keys = jax.random.split(key, N_GRP)
    starts = jax.vmap(shuffled_starts)(group_keys)
    offsets = jnp.arange(NOB, dtype=jnp.int32)
    owners = ((starts[:, :, None] + offsets[None, None, :]) % N_MEM).reshape(N_GRP, N_MEM * NOB)
    positions = jnp.arange(N_MEM * NOB, dtype=jnp.int32)
    earlier = positions[:, None] > positions[None, :]

    def slot_of(owner_row):
        same_owner = owner_row[:, None] == owner_row[None, :]
        return jnp.sum(same_owner & earlier, axis=1).astype(jnp.int32)
    slot_index = jax.vmap(slot_of)(owners)
    return (owners * NOB + slot_index).astype(jnp.int32)


def draw_task_slab(key, part):
    key = jax.random.fold_in(key, 23)
    popular_key, full_key, noise_key = jax.random.split(key, 3)
    demand_level = jax.random.randint(popular_key, (N_GRP, 1, SLABS), 0, 4, dtype=jnp.int32)
    complete_holder = jax.random.randint(full_key, (N_GRP, N_MEM, 1), 0, SLABS // SLABS_PER_MEMORY, dtype=jnp.int32)
    jitter_term = jax.random.randint(noise_key, (N_GRP, N_MEM, SLABS), 0, 1 << 18, dtype=jnp.int32)
    slab_position_index = jnp.arange(SLABS, dtype=jnp.int32)
    reward_boost = jnp.where((slab_position_index // SLABS_PER_MEMORY)[None, None, :] == complete_holder, 1 << 21, 0).astype(jnp.int32)
    ranking_marks = jitter_term + demand_level * (1 << 17) + reward_boost
    distinct = ranking_marks * SLABS + slab_position_index[None, None, :]
    picked = lax.top_k(distinct, VB)[1]
    return picked.astype(jnp.int32)


def block_levels(stream_key, extent, pieces, smallest, high):
    level = 1.0
    for dim, parts in pieces:
        draws = jax.random.uniform(jax.random.fold_in(jax.random.fold_in(stream_key, 6), dim), (parts,), jnp.float32, smallest / len(pieces), high / len(pieces))
        level = level * jnp.repeat(jnp.exp(draws), extent[dim] // parts).reshape((-1,) + (1,) * (len(extent) - 1 - dim))
    return level


def normal_values(key, shape, spread, most, cuts=(), held_as=jnp.bfloat16):
    values = spread * jax.random.normal(key, shape, jnp.float32)
    if cuts:
        values = values * block_levels(key, shape, cuts, -0.22, 0.18)
    return jnp.clip(values, -most, most).astype(held_as)


def setup_inputs(seed: int = 0) -> dict:
    key_list = jax.random.split(jax.random.key(seed), 6)
    t_store = normal_values(key_list[0], (N_GRP * N_MEM * NOB, OT, K), 1.0, 6.0, ((0, 1024),))
    v_blocks = normal_values(key_list[1], (N_GRP * N_MEM * VB, N, K), (K * N_GRP * N_MEM * VB // SLABS) ** -0.5, 0.0048828125, ((0, 1024),))
    block_id = jax.vmap(lambda own: jax.random.permutation(own, N_MEM))(jax.random.split(key_list[2], N_GRP)).reshape((N_GRP, N_MEM)).astype(jnp.int32)
    tile_home = draw_tile_home(jax.random.fold_in(key_list[5], 71), 0)
    task_slab = draw_task_slab(jax.random.fold_in(key_list[5], 71), 0)
    return {"t_store": t_store, "v_blocks": v_blocks, "block_id": block_id, "tile_home": tile_home, "task_slab": task_slab}


def reference(t_store, v_blocks, block_id, tile_home, task_slab):
    offsets = jnp.arange(NOB, dtype=jnp.int32)

    def accumulate(running, position):
        group_index = position // N_MEM
        member = position % N_MEM
        pair_q = block_id[group_index, member]
        places = tile_home[group_index, pair_q * NOB + offsets] + group_index * (N_MEM * NOB)
        column = t_store[places].reshape(NOB * OT, K).astype(jnp.float32)
        blocks = lax.dynamic_slice_in_dim(v_blocks, (position * VB).astype(jnp.int32), VB, 0).astype(jnp.float32)
        product = jnp.einsum("rk,bnk->rbn", column, blocks, precision=lax.Precision.HIGHEST)
        slab_rows = task_slab[group_index, member]
        return running.at[:, slab_rows, :].add(product), None

    start = jnp.zeros((NOB * OT, SLABS, N), jnp.float32)
    running = lax.scan(accumulate, start, jnp.arange(N_GRP * N_MEM, dtype=jnp.int32))[0]
    return running.reshape(NOB * OT, SLABS * N)
```

```python
import functools

import jax
import jax.numpy as jnp
from jax import lax
from jax.experimental import pallas as pl
from jax.experimental.pallas import tpu as pltpu
from jax.sharding import PartitionSpec as P

MESH = pl.DeviceIdType.MESH
XS = 4


def peer_step(i, ys):
    half = (i + 1) // 2
    return lax.rem(ys // 2 + jnp.where(i % 2 == 1, -half, half) + ys, ys)


def kernel(
    t_hbm, v_hbm, bid_hbm, home_hbm, slab_hbm, out_ref,
    t_v, v_v, send, recv, col, tiles, mine, other, core_in, mem_in, z_out, z_in,
    bid, home, slab, inv,
    in_sem, t_send_sem, t_recv_sem, core_sem, m_send_sem, m_recv_sem, z_send_sem, z_recv_sem,
):
    mems = lax.axis_size("mem")
    grps = lax.axis_size("grp")
    ys = mems // XS
    zs = grps // 2
    nob, ot = t_v.shape[0], t_v.shape[1]
    tasks = slab.shape[0]
    n = out_ref.shape[1]
    groups = zs // 4

    me = lax.axis_index("mem")
    grp = lax.axis_index("grp")
    y, x = me // XS, lax.rem(me, XS)
    z, core = grp // 2, lax.rem(grp, 2)

    def mem_peer(t):
        py = lax.rem(y + peer_step(t // XS, ys), ys)
        px = lax.rem(x + lax.rem(t, XS), XS)
        return py * XS + px

    own = mems - XS
    spans = ((0, own), (own + 1, mems))

    def over_peers(body):
        for lo, hi in spans:
            lax.fori_loop(lo, hi, lambda t, c: (body(t), c)[1], 0)

    loads = [
        pltpu.make_async_copy(src, dst, in_sem.at[i])
        for i, (src, dst) in enumerate(
            ((bid_hbm, bid), (home_hbm, home), (slab_hbm, slab), (t_hbm, t_v), (v_hbm, v_v))
        )
    ]
    for load in loads:
        load.start()

    barrier = pltpu.get_barrier_semaphore()
    over_peers(
        lambda t: pl.semaphore_signal(barrier, inc=1, device_id=(grp, mem_peer(t)), device_id_type=MESH)
    )
    sibling = z * 2 + 1 - core
    pl.semaphore_signal(barrier, inc=1, device_id=(sibling, me), device_id_type=MESH)

    def z_peer(k):
        return lax.rem(z + k, zs)

    def z_hello(k, c):
        pl.semaphore_signal(barrier, inc=1, device_id=(z_peer(k) * 2 + core, me), device_id_type=MESH)
        return c

    lax.fori_loop(1, zs, z_hello, 0)

    for load in loads[:4]:
        load.wait()

    def tile_for(p):
        q = bid[0, p]
        start = home[0, q * nob] // nob
        o = lax.rem(me - start + mems, mems)
        return lax.rem(home[0, q * nob + jnp.minimum(o, nob - 1)], nob)

    def pack(t):
        send[t] = t_v[tile_for(mem_peer(t))]

    over_peers(pack)
    recv[own] = t_v[tile_for(me)]

    pl.semaphore_wait(barrier, mems - 1 + 1 + zs - 1)

    def tile_copy(t):
        return pltpu.make_async_remote_copy(
            src_ref=send.at[t],
            dst_ref=recv.at[t],
            send_sem=t_send_sem.at[t],
            recv_sem=t_recv_sem.at[t],
            device_id=(grp, mem_peer(t)),
            device_id_type=MESH,
        )

    over_peers(lambda t: tile_copy(t).start())

    def locate(p, c):
        at = jnp.int32(tasks)
        for b in range(tasks):
            at = jnp.where(slab[b, 0, me] == p, b, at)
        inv[p] = at
        return c

    lax.fori_loop(0, mems, locate, 0)
    tiles[...] = jnp.zeros_like(tiles)
    loads[4].wait()

    over_peers(lambda t: tile_copy(t).wait_recv())

    first = home[0, bid[0, me] * nob] // nob
    for o in range(nob):
        src = lax.rem(first + o, mems)
        dy = lax.rem(y - src // XS + ys, ys)
        dx = lax.rem(x - lax.rem(src, XS) + XS, XS)
        e = dy - ys // 2
        t = jnp.where(e < 0, -2 * e - 1, 2 * e) * XS + dx
        col[o * ot:(o + 1) * ot, :] = recv[t]

    result = lax.dot_general(
        col[...], v_v[...], (((1,), (1,)), ((), ())), preferred_element_type=jnp.float32
    )

    row = lax.broadcasted_iota(jnp.int32, (8, n), 0)
    upper = lax.rem(row // 2, 2) == 1
    for b in range(tasks):
        for c in range(2):
            parts = []
            for k in range(groups):
                lo = result[k * 8:(k + 1) * 8, b * n:(b + 1) * n]
                hi = result[(k + groups) * 8:(k + groups + 1) * 8, b * n:(b + 1) * n]
                if c == 0:
                    parts.append(jnp.where(upper, pltpu.roll(hi, 2, 0), lo))
                else:
                    parts.append(jnp.where(upper, hi, pltpu.roll(lo, 6, 0)))
            tiles[c, b] = jnp.concatenate(parts, axis=1) if groups > 1 else parts[0]

    def spread(p, c):
        at = inv[p]
        other[p] = tiles[1 - core, at]
        mine[p] = tiles[core, at]
        return c

    lax.fori_loop(0, mems, spread, 0)

    to_sibling = pltpu.make_async_remote_copy(
        src_ref=other,
        dst_ref=core_in,
        send_sem=core_sem.at[0],
        recv_sem=core_sem.at[1],
        device_id=(sibling, me),
        device_id_type=MESH,
    )
    to_sibling.start()
    to_sibling.wait_recv()
    mine[...] = mine[...] + core_in[...]

    def slab_copy(t):
        p = mem_peer(t)
        return pltpu.make_async_remote_copy(
            src_ref=mine.at[p],
            dst_ref=mem_in.at[t],
            send_sem=m_send_sem.at[t],
            recv_sem=m_recv_sem.at[t],
            device_id=(grp, p),
            device_id_type=MESH,
        )

    over_peers(lambda t: slab_copy(t).start())
    mem_in[own] = mine[me]
    over_peers(lambda t: slab_copy(t).wait_recv())
    total = jnp.sum(mem_in[...], axis=0)
    for r in range(4):
        z_out[r] = total[2 * r:2 * r + 2, :]

    def rows_of(o):
        return lax.rem(o, 2) * 2 + jnp.where(o // 2 >= groups, 1, 0)

    def z_copy(k):
        to = z_peer(k)
        return pltpu.make_async_remote_copy(
            src_ref=z_out.at[rows_of(to)],
            dst_ref=z_in.at[k],
            send_sem=z_send_sem.at[k],
            recv_sem=z_recv_sem.at[k],
            device_id=(to * 2 + core, me),
            device_id_type=MESH,
        )

    lax.fori_loop(1, zs, lambda k, c: (z_copy(k).start(), c)[1], 0)
    z_in[0] = z_out[rows_of(z)]
    lax.fori_loop(1, zs, lambda k, c: (z_copy(k).wait_recv(), c)[1], 0)
    owned = jnp.sum(z_in[...], axis=0)
    group = lax.rem(z // 2, groups)
    out = owned[:, 0:n]
    for k in range(1, groups):
        out = jnp.where(group == k, owned[:, k * n:(k + 1) * n], out)
    out_ref[...] = out

    over_peers(lambda t: tile_copy(t).wait_send())
    to_sibling.wait_send()
    over_peers(lambda t: slab_copy(t).wait_send())
    lax.fori_loop(1, zs, lambda k, c: (z_copy(k).wait_send(), c)[1], 0)


def body(t_store, v_blocks, block_id, tile_home, task_slab):
    mems = lax.axis_size("mem")
    zs = lax.axis_size("grp") // 2
    nob, ot, width = t_store.shape
    tasks, n, _ = v_blocks.shape
    lanes = zs // 4 * n
    any_ref = pl.BlockSpec(memory_space=pl.ANY)
    dma = pltpu.SemaphoreType.DMA
    return pl.pallas_call(
        kernel,
        out_shape=jax.ShapeDtypeStruct((2, n), jnp.float32),
        in_specs=[any_ref] * 5,
        out_specs=pl.BlockSpec(memory_space=pltpu.VMEM),
        scratch_shapes=[
            pltpu.VMEM((nob, ot, width), jnp.bfloat16),
            pltpu.VMEM((tasks * n, width), jnp.bfloat16),
            pltpu.VMEM((mems, ot, width), jnp.bfloat16),
            pltpu.VMEM((mems, ot, width), jnp.bfloat16),
            pltpu.VMEM((nob * ot, width), jnp.bfloat16),
            pltpu.VMEM((2, tasks + 1, 8, lanes), jnp.float32),
            pltpu.VMEM((mems, 8, lanes), jnp.float32),
            pltpu.VMEM((mems, 8, lanes), jnp.float32),
            pltpu.VMEM((mems, 8, lanes), jnp.float32),
            pltpu.VMEM((mems, 8, lanes), jnp.float32),
            pltpu.VMEM((4, 2, lanes), jnp.float32),
            pltpu.VMEM((zs, 2, lanes), jnp.float32),
            pltpu.SMEM(block_id.shape, jnp.int32),
            pltpu.SMEM(tile_home.shape, jnp.int32),
            pltpu.SMEM((tasks, 1, mems), jnp.int32),
            pltpu.SMEM((mems,), jnp.int32),
            dma((5,)),
            dma((mems,)),
            dma((mems,)),
            dma((2,)),
            dma((mems,)),
            dma((mems,)),
            dma((zs,)),
            dma((zs,)),
        ],
        compiler_params=pltpu.CompilerParams(
            collective_id=0, has_side_effects=True, vmem_limit_bytes=60 * 1024 * 1024
        ),
        name="ladder",
    )(t_store, v_blocks.reshape(tasks * n, width), block_id, tile_home, jnp.transpose(task_slab, (2, 0, 1)))


def solution(mesh):
    return jax.shard_map(
        body,
        mesh=mesh,
        in_specs=(
            P(("grp", "mem"), None, None),
            P(("grp", "mem"), None, None),
            P("grp", None),
            P("grp", None),
            P("grp", None, None),
        ),
        out_specs=P("grp", "mem"),
        check_vma=False,
    )
```

```python
import functools

import jax
import jax.numpy as jnp
from jax import lax
from jax.experimental import pallas as pl
from jax.experimental.pallas import tpu as pltpu
from jax.sharding import PartitionSpec as P

MESH = pl.DeviceIdType.MESH
XS = 4


def offset(t, ys):
    g, s = t // (2 * XS), lax.rem(t, 2)
    dy = jnp.where(s == 0, ys // 2 - g, jnp.where(g == 0, 0, ys // 2 + g))
    return dy, lax.rem(t // 2, XS)


def step_of(dy, dx, ys):
    g = jnp.where(dy == 0, 0, jnp.where(dy <= ys // 2, ys // 2 - dy, dy - ys // 2))
    s = jnp.where((dy == 0) | (dy > ys // 2), 1, 0)
    return g * 2 * XS + dx * 2 + s


def kernel(
    t_hbm, v_hbm, bid_hbm, home_hbm, slab_hbm, out_ref,
    t_v, v_v, send, recv, col, tiles, mine, other, core_in, m_in, z_out, z_in,
    bid, home, slab, inv,
    in_sem, t_send_sem, t_recv_sem, c_send_sem, c_recv_sem, m_send_sem, m_recv_sem,
    z_send_sem, z_recv_sem, up_sem, down_sem,
):
    mems = lax.axis_size("mem")
    grps = lax.axis_size("grp")
    ys = mems // XS
    zs = grps // 2
    nob, ot = t_v.shape[0], t_v.shape[1]
    tasks = slab.shape[0]
    n = out_ref.shape[1]
    groups = zs // 4

    me = lax.axis_index("mem")
    grp = lax.axis_index("grp")
    y, x = me // XS, lax.rem(me, XS)
    z, core = grp // 2, lax.rem(grp, 2)

    def mem_peer(t):
        dy, dx = offset(t, ys)
        return lax.rem(y + dy, ys) * XS + lax.rem(x + dx, XS)

    own = 1

    def over_peers(body):
        for lo, hi in ((0, own), (own + 1, mems)):
            lax.fori_loop(lo, hi, lambda t, c: (body(t), c)[1], 0)

    loads = [
        pltpu.make_async_copy(src, dst, in_sem.at[i])
        for i, (src, dst) in enumerate(
            ((bid_hbm, bid), (home_hbm, home), (slab_hbm, slab), (t_hbm, t_v), (v_hbm, v_v))
        )
    ]
    for load in loads:
        load.start()

    barrier = pltpu.get_barrier_semaphore()
    over_peers(
        lambda t: pl.semaphore_signal(barrier, inc=1, device_id=(grp, mem_peer(t)), device_id_type=MESH)
    )
    sibling = z * 2 + 1 - core
    pl.semaphore_signal(barrier, inc=1, device_id=(sibling, me), device_id_type=MESH)

    def tell(to, semaphore):
        pl.semaphore_signal(semaphore, inc=1, device_id=(to * 2 + core, me), device_id_type=MESH)

    @pl.when(z > 0)
    def _():
        tell(z - 1, barrier)

    @pl.when(z < zs - 1)
    def _():
        tell(z + 1, barrier)

    for load in loads[:4]:
        load.wait()

    def tile_for(p):
        q = bid[0, p]
        start = home[0, q * nob] // nob
        o = lax.rem(me - start + mems, mems)
        return lax.rem(home[0, q * nob + jnp.minimum(o, nob - 1)], nob)

    def pack(t):
        send[t] = t_v[tile_for(mem_peer(t))]

    over_peers(pack)
    recv[own] = t_v[tile_for(me)]

    pl.semaphore_wait(barrier, mems + jnp.where(z > 0, 1, 0) + jnp.where(z < zs - 1, 1, 0))

    def tile_copy(t):
        return pltpu.make_async_remote_copy(
            src_ref=send.at[t],
            dst_ref=recv.at[t],
            send_sem=t_send_sem.at[t],
            recv_sem=t_recv_sem.at[t],
            device_id=(grp, mem_peer(t)),
            device_id_type=MESH,
        )

    over_peers(lambda t: tile_copy(t).start())

    @pl.when(z > 0)
    def _():
        pl.semaphore_wait(up_sem, 1)

    @pl.when(z < zs - 1)
    def _():
        tell(z + 1, up_sem)
        pl.semaphore_wait(down_sem, 1)

    @pl.when(z > 0)
    def _():
        tell(z - 1, down_sem)

    def locate(p, c):
        at = jnp.int32(tasks)
        for b in range(tasks):
            at = jnp.where(slab[b, 0, me] == p, b, at)
        inv[p] = at
        return c

    lax.fori_loop(0, mems, locate, 0)
    tiles[...] = jnp.zeros_like(tiles)
    loads[4].wait()

    over_peers(lambda t: tile_copy(t).wait_recv())

    first = home[0, bid[0, me] * nob] // nob
    for o in range(nob):
        src = lax.rem(first + o, mems)
        dy = lax.rem(y - src // XS + ys, ys)
        dx = lax.rem(x - lax.rem(src, XS) + XS, XS)
        t = step_of(dy, dx, ys)
        col[o * ot:(o + 1) * ot, :] = recv[t]

    result = lax.dot_general(
        col[...], v_v[...], (((1,), (1,)), ((), ())), preferred_element_type=jnp.float32
    )

    row = lax.broadcasted_iota(jnp.int32, (8, n), 0)
    upper = lax.rem(row // 2, 2) == 1
    for b in range(tasks):
        for c in range(2):
            parts = []
            for k in range(groups):
                lo = result[k * 8:(k + 1) * 8, b * n:(b + 1) * n]
                hi = result[(k + groups) * 8:(k + groups + 1) * 8, b * n:(b + 1) * n]
                if c == 0:
                    parts.append(jnp.where(upper, pltpu.roll(hi, 2, 0), lo))
                else:
                    parts.append(jnp.where(upper, hi, pltpu.roll(lo, 6, 0)))
            tiles[c, b] = jnp.concatenate(parts, axis=1) if groups > 1 else parts[0]

    def core_copy(dx):
        to = lax.rem(x + dx, XS)
        return pltpu.make_async_remote_copy(
            src_ref=other.at[to],
            dst_ref=core_in.at[to],
            send_sem=c_send_sem.at[dx],
            recv_sem=c_recv_sem.at[dx],
            device_id=(sibling, me),
            device_id_type=MESH,
        )

    x_order = (2, 1, 3, 0)
    y_all = sorted(range(ys), key=lambda dy: -min(dy, ys - dy))

    def m_copy(dx, dy):
        tx = lax.rem(x + dx, XS)
        ty = lax.rem(y + dy, ys)
        return pltpu.make_async_remote_copy(
            src_ref=mine.at[tx, ty],
            dst_ref=m_in.at[dx, dy],
            send_sem=m_send_sem.at[dx * ys + dy],
            recv_sem=m_recv_sem.at[dx * ys + dy],
            device_id=(grp, ty * XS + tx),
            device_id_type=MESH,
        )

    for dx in x_order:
        to = lax.rem(x + dx, XS)
        for r in range(ys):
            other[to, r] = tiles[1 - core, inv[r * XS + to]]
        core_copy(dx).start()
    for dx in x_order:
        to = lax.rem(x + dx, XS)
        for r in range(ys):
            mine[to, r] = tiles[core, inv[r * XS + to]]
    for dx in x_order:
        to = lax.rem(x + dx, XS)
        core_copy(dx).wait_recv()
        mine[to] = mine[to] + core_in[to]
        for dy in y_all:
            if dx or dy:
                m_copy(dx, dy).start()
    total = mine[x, y]
    for dx in x_order:
        for dy in y_all:
            if dx or dy:
                m_copy(dx, dy).wait_recv()
                total = total + m_in[dx, dy]
    for r in range(4):
        z_out[r] = total[2 * r:2 * r + 2, :]

    def rows_of(o):
        return lax.rem(o, 2) * 2 + jnp.where(o // 2 >= groups, 1, 0)

    def z_copy(k):
        to = lax.rem(z + k, zs)
        return pltpu.make_async_remote_copy(
            src_ref=z_out.at[rows_of(to)],
            dst_ref=z_in.at[k],
            send_sem=z_send_sem.at[k],
            recv_sem=z_recv_sem.at[k],
            device_id=(to * 2 + core, me),
            device_id_type=MESH,
        )

    lax.fori_loop(1, zs, lambda k, c: (z_copy(k).start(), c)[1], 0)
    z_in[0] = z_out[rows_of(z)]
    lax.fori_loop(1, zs, lambda k, c: (z_copy(k).wait_recv(), c)[1], 0)
    owned = jnp.sum(z_in[...], axis=0)
    group = lax.rem(z // 2, groups)
    out = owned[:, 0:n]
    for k in range(1, groups):
        out = jnp.where(group == k, owned[:, k * n:(k + 1) * n], out)
    out_ref[...] = out

    over_peers(lambda t: tile_copy(t).wait_send())
    for dx in x_order:
        core_copy(dx).wait_send()
        for dy in y_all:
            if dx or dy:
                m_copy(dx, dy).wait_send()
    lax.fori_loop(1, zs, lambda k, c: (z_copy(k).wait_send(), c)[1], 0)


def body(t_store, v_blocks, block_id, tile_home, task_slab):
    mems = lax.axis_size("mem")
    ys = mems // XS
    zs = lax.axis_size("grp") // 2
    nob, ot, width = t_store.shape
    tasks, n, _ = v_blocks.shape
    lanes = zs // 4 * n
    any_ref = pl.BlockSpec(memory_space=pl.ANY)
    dma = pltpu.SemaphoreType.DMA
    return pl.pallas_call(
        kernel,
        out_shape=jax.ShapeDtypeStruct((2, n), jnp.float32),
        in_specs=[any_ref] * 5,
        out_specs=pl.BlockSpec(memory_space=pltpu.VMEM),
        scratch_shapes=[
            pltpu.VMEM((nob, ot, width), jnp.bfloat16),
            pltpu.VMEM((tasks * n, width), jnp.bfloat16),
            pltpu.VMEM((mems, ot, width), jnp.bfloat16),
            pltpu.VMEM((mems, ot, width), jnp.bfloat16),
            pltpu.VMEM((nob * ot, width), jnp.bfloat16),
            pltpu.VMEM((2, tasks + 1, 8, lanes), jnp.float32),
            pltpu.VMEM((XS, ys, 8, lanes), jnp.float32),
            pltpu.VMEM((XS, ys, 8, lanes), jnp.float32),
            pltpu.VMEM((XS, ys, 8, lanes), jnp.float32),
            pltpu.VMEM((XS, ys, 8, lanes), jnp.float32),
            pltpu.VMEM((4, 2, lanes), jnp.float32),
            pltpu.VMEM((zs, 2, lanes), jnp.float32),
            pltpu.SMEM(block_id.shape, jnp.int32),
            pltpu.SMEM(tile_home.shape, jnp.int32),
            pltpu.SMEM((tasks, 1, mems), jnp.int32),
            pltpu.SMEM((mems,), jnp.int32),
            dma((5,)),
            dma((mems,)),
            dma((mems,)),
            dma((XS,)),
            dma((XS,)),
            dma((mems,)),
            dma((mems,)),
            dma((zs,)),
            dma((zs,)),
            pltpu.SemaphoreType.REGULAR,
            pltpu.SemaphoreType.REGULAR,
        ],
        compiler_params=pltpu.CompilerParams(
            collective_id=0, has_side_effects=True, vmem_limit_bytes=60 * 1024 * 1024
        ),
        name="ladder",
    )(t_store, v_blocks.reshape(tasks * n, width), block_id, tile_home, jnp.transpose(task_slab, (2, 0, 1)))


def solution(mesh):
    return jax.shard_map(
        body,
        mesh=mesh,
        in_specs=(
            P(("grp", "mem"), None, None),
            P(("grp", "mem"), None, None),
            P("grp", None),
            P("grp", None),
            P("grp", None, None),
        ),
        out_specs=P("grp", "mem"),
        check_vma=False,
    )
```

```python
import functools

import jax
import jax.numpy as jnp
from jax import lax
from jax.experimental import pallas as pl
from jax.experimental.pallas import tpu as pltpu
from jax.sharding import PartitionSpec as P

MESH = pl.DeviceIdType.MESH
XS = 4


def farthest_first(size):
    return sorted(range(size), key=lambda d: -min(d, size - d))


def kernel(
    t_hbm, v_hbm, bid_hbm, home_hbm, slab_hbm, out_ref,
    t_v, v_v, send, recv, col, tiles, mine, other, core_in, m_in, z_out, z_in,
    bid, home, slab, inv,
    in_sem, t_send_sem, t_recv_sem, c_send_sem, c_recv_sem, m_send_sem, m_recv_sem,
    z_send_sem, z_recv_sem, near_sem, above_sem, up_sem, all_sem,
):
    mems = lax.axis_size("mem")
    grps = lax.axis_size("grp")
    ys = mems // XS
    zs = grps // 2
    nob, ot = t_v.shape[0], t_v.shape[1]
    tasks = slab.shape[0]
    n = out_ref.shape[1]
    groups = zs // 4

    me = lax.axis_index("mem")
    grp = lax.axis_index("grp")
    y, x = me // XS, lax.rem(me, XS)
    z, core = grp // 2, lax.rem(grp, 2)

    at_y = [lax.rem(y + dy, ys) for dy in range(ys)]
    at_x = [lax.rem(x + dx, XS) for dx in range(XS)]
    x_order = farthest_first(XS)
    y_order = farthest_first(ys)

    def mem_peer(dy, dx):
        return at_y[dy] * XS + at_x[dx]

    barrier = pltpu.get_barrier_semaphore()
    near = [(dy, dx) for dx in x_order for dy in (1, ys - 1, 0) if dy or dx]
    for dy, dx in near:
        pl.semaphore_signal(barrier, inc=1, device_id=(grp, mem_peer(dy, dx)), device_id_type=MESH)
    sibling = z * 2 + 1 - core
    pl.semaphore_signal(barrier, inc=1, device_id=(sibling, me), device_id_type=MESH)

    def tell(to, semaphore):
        pl.semaphore_signal(semaphore, inc=1, device_id=(to * 2 + core, me), device_id_type=MESH)

    @pl.when(z < zs - 1)
    def _():
        tell(z + 1, barrier)

    loads = [
        pltpu.make_async_copy(src, dst, in_sem.at[i])
        for i, (src, dst) in enumerate(
            ((t_hbm, t_v), (home_hbm, home), (bid_hbm, bid), (slab_hbm, slab), (v_hbm, v_v))
        )
    ]
    for load in loads[:3]:
        load.start()

    for load in loads[:3]:
        load.wait()
    for load in loads[3:]:
        load.start()

    def tile_for(p):
        q = bid[0, p]
        start = home[0, q * nob] // nob
        o = lax.rem(me - start + mems, mems)
        return lax.rem(home[0, q * nob + jnp.minimum(o, nob - 1)], nob)

    def tile_copy(dy, dx):
        slot = dy * XS + dx
        return pltpu.make_async_remote_copy(
            src_ref=send.at[slot],
            dst_ref=recv.at[slot],
            send_sem=t_send_sem.at[slot],
            recv_sem=t_recv_sem.at[slot],
            device_id=(grp, mem_peer(dy, dx)),
            device_id_type=MESH,
        )

    pl.semaphore_wait(barrier, len(near) + 1 + jnp.where(z > 0, 1, 0))

    @pl.when(z > 0)
    def _():
        tell(z - 1, above_sem)

    def tell_rows(d):
        for dy in (1, ys - 1):
            pl.semaphore_signal(near_sem.at[d], inc=1, device_id=(grp, mem_peer(dy, 0)), device_id_type=MESH)

    tell_rows(1)
    half = ys // 2
    last = sorted({half, half - 1, ys - half + 1} - {1, ys - 1}, key=lambda d: -min(d, ys - d))
    plan = [near]
    plan += [[(dy, dx) for dx in x_order for dy in (d, ys - d)] for d in range(2, half - 1)]
    plan += [[(dy, dx) for dx in x_order for dy in last]]
    sent = []
    known = 1
    for rows in plan:
        for d in range(known + 1, max(min(dy, ys - dy) for dy, _ in rows) + 1):
            pl.semaphore_wait(near_sem.at[d - 1], 2)
            if d < half:
                tell_rows(d)
            known = d
        for dy, dx in rows:
            send[dy * XS + dx] = t_v[tile_for(mem_peer(dy, dx))]
            tile_copy(dy, dx).start()
        sent += rows
    recv[0] = t_v[tile_for(me)]

    @pl.when(z < zs - 1)
    def _():
        pl.semaphore_wait(above_sem, 1)

    @pl.when(z > 0)
    def _():
        pl.semaphore_wait(up_sem, 1)

    @pl.when(z < zs - 1)
    def _():
        tell(z + 1, up_sem)

    @pl.when(z == zs - 1)
    def _():
        for to in range(zs - 1):
            tell(to, all_sem)

    def locate(p, c):
        at = jnp.int32(tasks)
        for b in range(tasks):
            at = jnp.where(slab[b, 0, me] == p, b, at)
        inv[p] = at
        return c

    loads[3].wait()
    lax.fori_loop(0, mems, locate, 0)
    tiles[...] = jnp.zeros_like(tiles)
    loads[4].wait()

    @pl.when(z < zs - 1)
    def _():
        pl.semaphore_wait(all_sem, 1)

    for dy, dx in sent:
        tile_copy(dy, dx).wait_recv()

    first = home[0, bid[0, me] * nob] // nob
    for o in range(nob):
        src = lax.rem(first + o, mems)
        dy = lax.rem(y - src // XS + ys, ys)
        dx = lax.rem(x - lax.rem(src, XS) + XS, XS)
        t = dy * XS + dx
        col[o * ot:(o + 1) * ot, :] = recv[t]

    result = lax.dot_general(
        col[...], v_v[...], (((1,), (1,)), ((), ())), preferred_element_type=jnp.float32
    )

    row = lax.broadcasted_iota(jnp.int32, (8, n), 0)
    upper = lax.rem(row // 2, 2) == 1
    for b in range(tasks):
        for c in range(2):
            parts = []
            for k in range(groups):
                lo = result[k * 8:(k + 1) * 8, b * n:(b + 1) * n]
                hi = result[(k + groups) * 8:(k + groups + 1) * 8, b * n:(b + 1) * n]
                if c == 0:
                    parts.append(jnp.where(upper, pltpu.roll(hi, 2, 0), lo))
                else:
                    parts.append(jnp.where(upper, hi, pltpu.roll(lo, 6, 0)))
            tiles[c, b] = jnp.concatenate(parts, axis=1) if groups > 1 else parts[0]

    def core_copy(dx):
        to = at_x[dx]
        return pltpu.make_async_remote_copy(
            src_ref=other.at[to],
            dst_ref=core_in.at[to],
            send_sem=c_send_sem.at[dx],
            recv_sem=c_recv_sem.at[dx],
            device_id=(sibling, me),
            device_id_type=MESH,
        )

    def m_copy(dx, dy):
        tx, ty = at_x[dx], at_y[dy]
        return pltpu.make_async_remote_copy(
            src_ref=mine.at[tx, ty],
            dst_ref=m_in.at[dx, dy],
            send_sem=m_send_sem.at[dx * ys + dy],
            recv_sem=m_recv_sem.at[dx * ys + dy],
            device_id=(grp, ty * XS + tx),
            device_id_type=MESH,
        )

    for dx in x_order:
        to = at_x[dx]
        for r in range(ys):
            other[to, r] = tiles[1 - core, inv[r * XS + to]]
        core_copy(dx).start()
    for dx in x_order:
        to = at_x[dx]
        for r in range(ys):
            mine[to, r] = tiles[core, inv[r * XS + to]]
    for dx in x_order:
        to = at_x[dx]
        core_copy(dx).wait_recv()
        mine[to] = mine[to] + core_in[to]
        for dy in y_order:
            if dx or dy:
                m_copy(dx, dy).start()
    total = mine[x, y]
    for dx in x_order:
        for dy in y_order:
            if dx or dy:
                m_copy(dx, dy).wait_recv()
                total = total + m_in[dx, dy]
    for r in range(4):
        z_out[r] = total[2 * r:2 * r + 2, :]

    def rows_of(o):
        return lax.rem(o, 2) * 2 + jnp.where(o // 2 >= groups, 1, 0)

    def other_plane(i):
        return i - jnp.where(i > z, 0, 1)

    def z_copy(i):
        to = other_plane(i)
        return pltpu.make_async_remote_copy(
            src_ref=z_out.at[rows_of(to)],
            dst_ref=z_in.at[z],
            send_sem=z_send_sem.at[to],
            recv_sem=z_recv_sem.at[z],
            device_id=(to * 2 + core, me),
            device_id_type=MESH,
        )

    def z_arrival(i):
        src = other_plane(i)
        return pltpu.make_async_remote_copy(
            src_ref=z_out.at[0],
            dst_ref=z_in.at[src],
            send_sem=z_send_sem.at[src],
            recv_sem=z_recv_sem.at[src],
            device_id=(src * 2 + core, me),
            device_id_type=MESH,
        )

    for i in range(1, zs):
        z_copy(i).start()
    owned = z_out[rows_of(z)]
    for i in range(1, zs):
        z_arrival(i).wait_recv()
        owned = owned + z_in[other_plane(i)]
    group = lax.rem(z // 2, groups)
    out = owned[:, 0:n]
    for k in range(1, groups):
        out = jnp.where(group == k, owned[:, k * n:(k + 1) * n], out)
    out_ref[...] = out

    for dy, dx in sent:
        tile_copy(dy, dx).wait_send()
    for dx in x_order:
        core_copy(dx).wait_send()
        for dy in y_order:
            if dx or dy:
                m_copy(dx, dy).wait_send()
    for i in range(1, zs):
        z_copy(i).wait_send()


def body(t_store, v_blocks, block_id, tile_home, task_slab):
    mems = lax.axis_size("mem")
    ys = mems // XS
    zs = lax.axis_size("grp") // 2
    nob, ot, width = t_store.shape
    tasks, n, _ = v_blocks.shape
    lanes = zs // 4 * n
    any_ref = pl.BlockSpec(memory_space=pl.ANY)
    dma = pltpu.SemaphoreType.DMA
    return pl.pallas_call(
        kernel,
        out_shape=jax.ShapeDtypeStruct((2, n), jnp.float32),
        in_specs=[any_ref] * 5,
        out_specs=pl.BlockSpec(memory_space=pltpu.VMEM),
        scratch_shapes=[
            pltpu.VMEM((nob, ot, width), jnp.bfloat16),
            pltpu.VMEM((tasks * n, width), jnp.bfloat16),
            pltpu.VMEM((mems, ot, width), jnp.bfloat16),
            pltpu.VMEM((mems, ot, width), jnp.bfloat16),
            pltpu.VMEM((nob * ot, width), jnp.bfloat16),
            pltpu.VMEM((2, tasks + 1, 8, lanes), jnp.float32),
            pltpu.VMEM((XS, ys, 8, lanes), jnp.float32),
            pltpu.VMEM((XS, ys, 8, lanes), jnp.float32),
            pltpu.VMEM((XS, ys, 8, lanes), jnp.float32),
            pltpu.VMEM((XS, ys, 8, lanes), jnp.float32),
            pltpu.VMEM((4, 2, lanes), jnp.float32),
            pltpu.VMEM((zs, 2, lanes), jnp.float32),
            pltpu.SMEM(block_id.shape, jnp.int32),
            pltpu.SMEM(tile_home.shape, jnp.int32),
            pltpu.SMEM((tasks, 1, mems), jnp.int32),
            pltpu.SMEM((mems,), jnp.int32),
            dma((5,)),
            dma((mems,)),
            dma((mems,)),
            dma((XS,)),
            dma((XS,)),
            dma((mems,)),
            dma((mems,)),
            dma((zs,)),
            dma((zs,)),
            pltpu.SemaphoreType.REGULAR((ys // 2,)),
            pltpu.SemaphoreType.REGULAR,
            pltpu.SemaphoreType.REGULAR,
            pltpu.SemaphoreType.REGULAR,
        ],
        compiler_params=pltpu.CompilerParams(
            collective_id=0, has_side_effects=True, vmem_limit_bytes=60 * 1024 * 1024
        ),
        name="ladder",
    )(t_store, v_blocks.reshape(tasks * n, width), block_id, tile_home, jnp.transpose(task_slab, (2, 0, 1)))


def solution(mesh):
    return jax.shard_map(
        body,
        mesh=mesh,
        in_specs=(
            P(("grp", "mem"), None, None),
            P(("grp", "mem"), None, None),
            P("grp", None),
            P("grp", None),
            P("grp", None, None),
        ),
        out_specs=P("grp", "mem"),
        check_vma=False,
    )
```

```python
import functools

import jax
import jax.numpy as jnp
from jax import lax
from jax.experimental import pallas as pl
from jax.experimental.pallas import tpu as pltpu
from jax.sharding import PartitionSpec as P

MESH = pl.DeviceIdType.MESH
XS = 4


def farthest_first(size):
    return sorted(range(size), key=lambda d: -min(d, size - d))


def kernel(
    t_hbm, v_hbm, bid_hbm, home_hbm, slab_hbm, out_ref,
    t_v, v_v, send, recv, col, tiles, mine, other, core_in, m_in, z_out, z_in,
    bid, home, slab, inv,
    in_sem, t_send_sem, t_recv_sem, c_send_sem, c_recv_sem, m_send_sem, m_recv_sem,
    z_send_sem, z_recv_sem, near_sem, above_sem, up_sem, all_sem,
):
    mems = lax.axis_size("mem")
    grps = lax.axis_size("grp")
    ys = mems // XS
    zs = grps // 2
    nob, ot = t_v.shape[0], t_v.shape[1]
    tasks = slab.shape[0]
    n = out_ref.shape[1]
    groups = zs // 4

    me = lax.axis_index("mem")
    grp = lax.axis_index("grp")
    y, x = me // XS, lax.rem(me, XS)
    z, core = grp // 2, lax.rem(grp, 2)

    at_y = [lax.rem(y + dy, ys) for dy in range(ys)]
    at_x = [lax.rem(x + dx, XS) for dx in range(XS)]
    x_order = farthest_first(XS)

    def mem_peer(dy, dx):
        return at_y[dy] * XS + at_x[dx]

    barrier = pltpu.get_barrier_semaphore()
    near = [(dy, dx) for dx in x_order for dy in (1, ys - 1, 0) if dy or dx]
    for dy, dx in near:
        pl.semaphore_signal(barrier, inc=1, device_id=(grp, mem_peer(dy, dx)), device_id_type=MESH)
    sibling = z * 2 + 1 - core
    pl.semaphore_signal(barrier, inc=1, device_id=(sibling, me), device_id_type=MESH)

    def tell(to, semaphore):
        pl.semaphore_signal(semaphore, inc=1, device_id=(to * 2 + core, me), device_id_type=MESH)

    @pl.when(z < zs - 1)
    def _():
        tell(z + 1, barrier)

    loads = [
        pltpu.make_async_copy(src, dst, in_sem.at[i])
        for i, (src, dst) in enumerate(
            ((t_hbm, t_v), (home_hbm, home), (bid_hbm, bid), (slab_hbm, slab), (v_hbm, v_v))
        )
    ]
    for load in loads[:3]:
        load.start()

    for load in loads[:3]:
        load.wait()
    for load in loads[3:]:
        load.start()

    def tile_for(p):
        q = bid[0, p]
        start = home[0, q * nob] // nob
        o = lax.rem(me - start + mems, mems)
        return lax.rem(home[0, q * nob + jnp.minimum(o, nob - 1)], nob)

    def tile_copy(dy, dx):
        slot = dy * XS + dx
        return pltpu.make_async_remote_copy(
            src_ref=send.at[slot],
            dst_ref=recv.at[slot],
            send_sem=t_send_sem.at[slot],
            recv_sem=t_recv_sem.at[slot],
            device_id=(grp, mem_peer(dy, dx)),
            device_id_type=MESH,
        )

    pl.semaphore_wait(barrier, len(near) + 1 + jnp.where(z > 0, 1, 0))

    @pl.when(z > 0)
    def _():
        tell(z - 1, above_sem)

    def tell_rows(d):
        for dy in (1, ys - 1):
            pl.semaphore_signal(near_sem.at[d], inc=1, device_id=(grp, mem_peer(dy, 0)), device_id_type=MESH)

    tell_rows(1)
    half = ys // 2
    last = sorted({half, half - 1, ys - half + 1} - {1, ys - 1}, key=lambda d: -min(d, ys - d))
    plan = [near]
    plan += [[(dy, dx) for dx in x_order for dy in (d, ys - d)] for d in range(2, half - 1)]
    plan += [[(dy, dx) for dx in x_order for dy in last]]
    sent = []
    known = 1
    for rows in plan:
        for d in range(known + 1, max(min(dy, ys - dy) for dy, _ in rows) + 1):
            pl.semaphore_wait(near_sem.at[d - 1], 2)
            if d < half:
                tell_rows(d)
            known = d
        for dy, dx in rows:
            send[dy * XS + dx] = t_v[tile_for(mem_peer(dy, dx))]
            tile_copy(dy, dx).start()
        sent += rows
    recv[0] = t_v[tile_for(me)]

    @pl.when(z < zs - 1)
    def _():
        pl.semaphore_wait(above_sem, 1)

    @pl.when(z > 0)
    def _():
        pl.semaphore_wait(up_sem, 1)

    @pl.when(z < zs - 1)
    def _():
        tell(z + 1, up_sem)

    @pl.when(z == zs - 1)
    def _():
        for to in range(zs - 1):
            tell(to, all_sem)

    def locate(p, c):
        at = jnp.int32(tasks)
        for b in range(tasks):
            at = jnp.where(slab[b, 0, me] == p, b, at)
        inv[p] = at
        return c

    loads[3].wait()
    lax.fori_loop(0, mems, locate, 0)
    tiles[...] = jnp.zeros_like(tiles)
    loads[4].wait()

    @pl.when(z < zs - 1)
    def _():
        pl.semaphore_wait(all_sem, 1)

    for dy, dx in sent:
        tile_copy(dy, dx).wait_recv()

    first = home[0, bid[0, me] * nob] // nob
    for o in range(nob):
        src = lax.rem(first + o, mems)
        dy = lax.rem(y - src // XS + ys, ys)
        dx = lax.rem(x - lax.rem(src, XS) + XS, XS)
        t = dy * XS + dx
        col[o * ot:(o + 1) * ot, :] = recv[t]

    result = lax.dot_general(
        col[...], v_v[...], (((1,), (1,)), ((), ())), preferred_element_type=jnp.float32
    )

    row = lax.broadcasted_iota(jnp.int32, (8, n), 0)
    upper = lax.rem(row // 2, 2) == 1
    for b in range(tasks):
        for c in range(2):
            parts = []
            for k in range(groups):
                lo = result[k * 8:(k + 1) * 8, b * n:(b + 1) * n]
                hi = result[(k + groups) * 8:(k + groups + 1) * 8, b * n:(b + 1) * n]
                if c == 0:
                    parts.append(jnp.where(upper, pltpu.roll(hi, 2, 0), lo))
                else:
                    parts.append(jnp.where(upper, hi, pltpu.roll(lo, 6, 0)))
            tiles[c, b] = jnp.concatenate(parts, axis=1) if groups > 1 else parts[0]

    def core_copy(tx):
        return pltpu.make_async_remote_copy(
            src_ref=other.at[tx],
            dst_ref=core_in.at[tx],
            send_sem=c_send_sem.at[tx],
            recv_sem=c_recv_sem.at[tx],
            device_id=(sibling, me),
            device_id_type=MESH,
        )

    def m_copy(p):
        return pltpu.make_async_remote_copy(
            src_ref=mine.at[p % XS, p // XS],
            dst_ref=m_in.at[me],
            send_sem=m_send_sem.at[p],
            recv_sem=m_recv_sem.at[me],
            device_id=(grp, p),
            device_id_type=MESH,
        )

    def m_arrival(p):
        return pltpu.make_async_remote_copy(
            src_ref=mine.at[p % XS, p // XS],
            dst_ref=m_in.at[p],
            send_sem=m_send_sem.at[p],
            recv_sem=m_recv_sem.at[p],
            device_id=(grp, p),
            device_id_type=MESH,
        )

    columns, lines = farthest_first(XS)[::-1], farthest_first(ys)[::-1]
    for tx in columns:
        for r in range(ys):
            other[tx, r] = tiles[1 - core, inv[r * XS + tx]]
        core_copy(tx).start()
    for tx in columns:
        for r in range(ys):
            mine[tx, r] = tiles[core, inv[r * XS + tx]]
    for tx in columns:
        core_copy(tx).wait_recv()
        mine[tx] = mine[tx] + core_in[tx]
        for ty in lines:
            @pl.when(me != ty * XS + tx)
            def _():
                m_copy(ty * XS + tx).start()
    m_in[me] = mine[x, y]
    for p in range(mems):
        @pl.when(me != p)
        def _():
            m_arrival(p).wait_recv()
    total = jnp.sum(m_in[...], axis=0)
    for r in range(4):
        z_out[r] = total[2 * r:2 * r + 2, :]

    def rows_of(o):
        return lax.rem(o, 2) * 2 + jnp.where(o // 2 >= groups, 1, 0)

    def other_plane(i):
        return i - jnp.where(i > z, 0, 1)

    def z_copy(i):
        to = other_plane(i)
        return pltpu.make_async_remote_copy(
            src_ref=z_out.at[rows_of(to)],
            dst_ref=z_in.at[z],
            send_sem=z_send_sem.at[to],
            recv_sem=z_recv_sem.at[z],
            device_id=(to * 2 + core, me),
            device_id_type=MESH,
        )

    def z_arrival(i):
        src = other_plane(i)
        return pltpu.make_async_remote_copy(
            src_ref=z_out.at[0],
            dst_ref=z_in.at[src],
            send_sem=z_send_sem.at[src],
            recv_sem=z_recv_sem.at[src],
            device_id=(src * 2 + core, me),
            device_id_type=MESH,
        )

    for i in range(1, zs):
        z_copy(i).start()
    owned = z_out[rows_of(z)]
    for i in range(1, zs):
        z_arrival(i).wait_recv()
        owned = owned + z_in[other_plane(i)]
    group = lax.rem(z // 2, groups)
    out = owned[:, 0:n]
    for k in range(1, groups):
        out = jnp.where(group == k, owned[:, k * n:(k + 1) * n], out)
    out_ref[...] = out

    for dy, dx in sent:
        tile_copy(dy, dx).wait_send()
    for tx in columns:
        core_copy(tx).wait_send()
    for p in range(mems):
        @pl.when(me != p)
        def _():
            m_copy(p).wait_send()
    for i in range(1, zs):
        z_copy(i).wait_send()


def body(t_store, v_blocks, block_id, tile_home, task_slab):
    mems = lax.axis_size("mem")
    ys = mems // XS
    zs = lax.axis_size("grp") // 2
    nob, ot, width = t_store.shape
    tasks, n, _ = v_blocks.shape
    lanes = zs // 4 * n
    any_ref = pl.BlockSpec(memory_space=pl.ANY)
    dma = pltpu.SemaphoreType.DMA
    return pl.pallas_call(
        kernel,
        out_shape=jax.ShapeDtypeStruct((2, n), jnp.float32),
        in_specs=[any_ref] * 5,
        out_specs=pl.BlockSpec(memory_space=pltpu.VMEM),
        scratch_shapes=[
            pltpu.VMEM((nob, ot, width), jnp.bfloat16),
            pltpu.VMEM((tasks * n, width), jnp.bfloat16),
            pltpu.VMEM((mems, ot, width), jnp.bfloat16),
            pltpu.VMEM((mems, ot, width), jnp.bfloat16),
            pltpu.VMEM((nob * ot, width), jnp.bfloat16),
            pltpu.VMEM((2, tasks + 1, 8, lanes), jnp.float32),
            pltpu.VMEM((XS, ys, 8, lanes), jnp.float32),
            pltpu.VMEM((XS, ys, 8, lanes), jnp.float32),
            pltpu.VMEM((XS, ys, 8, lanes), jnp.float32),
            pltpu.VMEM((mems, 8, lanes), jnp.float32),
            pltpu.VMEM((4, 2, lanes), jnp.float32),
            pltpu.VMEM((zs, 2, lanes), jnp.float32),
            pltpu.SMEM(block_id.shape, jnp.int32),
            pltpu.SMEM(tile_home.shape, jnp.int32),
            pltpu.SMEM((tasks, 1, mems), jnp.int32),
            pltpu.SMEM((mems,), jnp.int32),
            dma((5,)),
            dma((mems,)),
            dma((mems,)),
            dma((XS,)),
            dma((XS,)),
            dma((mems,)),
            dma((mems,)),
            dma((zs,)),
            dma((zs,)),
            pltpu.SemaphoreType.REGULAR((ys // 2,)),
            pltpu.SemaphoreType.REGULAR,
            pltpu.SemaphoreType.REGULAR,
            pltpu.SemaphoreType.REGULAR,
        ],
        compiler_params=pltpu.CompilerParams(
            collective_id=0, has_side_effects=True, vmem_limit_bytes=60 * 1024 * 1024
        ),
        name="ladder",
    )(t_store, v_blocks.reshape(tasks * n, width), block_id, tile_home, jnp.transpose(task_slab, (2, 0, 1)))


def solution(mesh):
    return jax.shard_map(
        body,
        mesh=mesh,
        in_specs=(
            P(("grp", "mem"), None, None),
            P(("grp", "mem"), None, None),
            P("grp", None),
            P("grp", None),
            P("grp", None, None),
        ),
        out_specs=P("grp", "mem"),
        check_vma=False,
    )
```

```python
import functools

import jax
import jax.numpy as jnp
from jax import lax
from jax.experimental import pallas as pl
from jax.experimental.pallas import tpu as pltpu
from jax.sharding import PartitionSpec as P

MESH = pl.DeviceIdType.MESH
XS = 4


def farthest_first(size):
    return sorted(range(size), key=lambda d: -min(d, size - d))


def kernel(
    t_hbm, v_hbm, bid_hbm, home_hbm, slab_hbm, out_ref,
    t_v, v_v, send, recv, col, tiles, mine, other, core_in, m_in, z_out, z_in,
    bid, home, slab, inv,
    in_sem, t_send_sem, t_recv_sem, c_send_sem, c_recv_sem, m_send_sem, m_recv_sem,
    z_send_sem, z_recv_sem, near_sem, above_sem, up_sem, all_sem,
):
    mems = lax.axis_size("mem")
    grps = lax.axis_size("grp")
    ys = mems // XS
    zs = grps // 2
    nob, ot = t_v.shape[0], t_v.shape[1]
    tasks = slab.shape[0]
    n = out_ref.shape[1]
    groups = zs // 4

    me = lax.axis_index("mem")
    grp = lax.axis_index("grp")
    y, x = me // XS, lax.rem(me, XS)
    z, core = grp // 2, lax.rem(grp, 2)

    at_y = [lax.rem(y + dy, ys) for dy in range(ys)]
    at_x = [lax.rem(x + dx, XS) for dx in range(XS)]
    x_order = farthest_first(XS)

    def mem_peer(dy, dx):
        return at_y[dy] * XS + at_x[dx]

    barrier = pltpu.get_barrier_semaphore()
    near = [(dy, dx) for dx in x_order for dy in (1, ys - 1, 0) if dy or dx]
    for dy, dx in near:
        pl.semaphore_signal(barrier, inc=1, device_id=(grp, mem_peer(dy, dx)), device_id_type=MESH)
    sibling = z * 2 + 1 - core
    pl.semaphore_signal(barrier, inc=1, device_id=(sibling, me), device_id_type=MESH)

    def tell(to, semaphore):
        pl.semaphore_signal(semaphore, inc=1, device_id=(to * 2 + core, me), device_id_type=MESH)

    @pl.when(z < zs - 1)
    def _():
        tell(z + 1, barrier)

    loads = [
        pltpu.make_async_copy(src, dst, in_sem.at[i])
        for i, (src, dst) in enumerate(
            ((t_hbm, t_v), (home_hbm, home), (bid_hbm, bid), (slab_hbm, slab), (v_hbm, v_v))
        )
    ]
    for load in loads[:3]:
        load.start()

    for load in loads[:3]:
        load.wait()
    for load in loads[3:]:
        load.start()

    def tile_for(p):
        q = bid[0, p]
        start = home[0, q * nob] // nob
        o = lax.rem(me - start + mems, mems)
        return lax.rem(home[0, q * nob + jnp.minimum(o, nob - 1)], nob)

    def tile_copy(dy, dx):
        slot = dy * XS + dx
        return pltpu.make_async_remote_copy(
            src_ref=send.at[slot],
            dst_ref=recv.at[slot],
            send_sem=t_send_sem,
            recv_sem=t_recv_sem,
            device_id=(grp, mem_peer(dy, dx)),
            device_id_type=MESH,
        )

    def tile_all():
        return pltpu.make_async_remote_copy(
            src_ref=send.at[1:],
            dst_ref=recv.at[1:],
            send_sem=t_send_sem,
            recv_sem=t_recv_sem,
            device_id=(grp, me),
            device_id_type=MESH,
        )

    pl.semaphore_wait(barrier, len(near) + 1 + jnp.where(z > 0, 1, 0))

    @pl.when(z > 0)
    def _():
        tell(z - 1, above_sem)

    def tell_rows(d):
        for dy in (1, ys - 1):
            pl.semaphore_signal(near_sem.at[d], inc=1, device_id=(grp, mem_peer(dy, 0)), device_id_type=MESH)

    tell_rows(1)
    half = ys // 2
    last = sorted({half, half - 1, ys - half + 1} - {1, ys - 1}, key=lambda d: -min(d, ys - d))
    plan = [near]
    plan += [[(dy, dx) for dx in x_order for dy in (d, ys - d)] for d in range(2, half - 1)]
    plan += [[(dy, dx) for dx in x_order for dy in last]]
    known = 1
    for rows in plan:
        for d in range(known + 1, max(min(dy, ys - dy) for dy, _ in rows) + 1):
            pl.semaphore_wait(near_sem.at[d - 1], 2)
            if d < half:
                tell_rows(d)
            known = d
        for dy, dx in rows:
            send[dy * XS + dx] = t_v[tile_for(mem_peer(dy, dx))]
            tile_copy(dy, dx).start()
    recv[0] = t_v[tile_for(me)]

    @pl.when(z < zs - 1)
    def _():
        pl.semaphore_wait(above_sem, 1)

    @pl.when(z > 0)
    def _():
        pl.semaphore_wait(up_sem, 1)

    @pl.when(z < zs - 1)
    def _():
        tell(z + 1, up_sem)

    @pl.when(z == zs - 1)
    def _():
        for to in range(zs - 1):
            tell(to, all_sem)

    def locate(p, c):
        at = jnp.int32(tasks)
        for b in range(tasks):
            at = jnp.where(slab[b, 0, me] == p, b, at)
        inv[p] = at
        return c

    loads[3].wait()
    lax.fori_loop(0, mems, locate, 0)
    tiles[...] = jnp.zeros_like(tiles)
    loads[4].wait()

    @pl.when(z < zs - 1)
    def _():
        pl.semaphore_wait(all_sem, 1)

    tile_all().wait_recv()

    first = home[0, bid[0, me] * nob] // nob
    for o in range(nob):
        src = lax.rem(first + o, mems)
        dy = lax.rem(y - src // XS + ys, ys)
        dx = lax.rem(x - lax.rem(src, XS) + XS, XS)
        t = dy * XS + dx
        col[o * ot:(o + 1) * ot, :] = recv[t]

    result = lax.dot_general(
        col[...], v_v[...], (((1,), (1,)), ((), ())), preferred_element_type=jnp.float32
    )

    row = lax.broadcasted_iota(jnp.int32, (8, n), 0)
    upper = lax.rem(row // 2, 2) == 1
    for b in range(tasks):
        for c in range(2):
            parts = []
            for k in range(groups):
                lo = result[k * 8:(k + 1) * 8, b * n:(b + 1) * n]
                hi = result[(k + groups) * 8:(k + groups + 1) * 8, b * n:(b + 1) * n]
                if c == 0:
                    parts.append(jnp.where(upper, pltpu.roll(hi, 2, 0), lo))
                else:
                    parts.append(jnp.where(upper, hi, pltpu.roll(lo, 6, 0)))
            tiles[c, b] = jnp.concatenate(parts, axis=1) if groups > 1 else parts[0]

    def core_copy(tx):
        return pltpu.make_async_remote_copy(
            src_ref=other.at[tx],
            dst_ref=core_in.at[tx],
            send_sem=c_send_sem,
            recv_sem=c_recv_sem.at[tx],
            device_id=(sibling, me),
            device_id_type=MESH,
        )

    def m_copy(p):
        return pltpu.make_async_remote_copy(
            src_ref=mine.at[p % XS, p // XS],
            dst_ref=m_in.at[me],
            send_sem=m_send_sem,
            recv_sem=m_recv_sem,
            device_id=(grp, p),
            device_id_type=MESH,
        )

    def m_all():
        return pltpu.make_async_remote_copy(
            src_ref=m_in.at[1:],
            dst_ref=m_in.at[1:],
            send_sem=m_send_sem,
            recv_sem=m_recv_sem,
            device_id=(grp, me),
            device_id_type=MESH,
        )

    columns, lines = farthest_first(XS)[::-1], farthest_first(ys)[::-1]
    for tx in columns:
        for r in range(ys):
            other[tx, r] = tiles[1 - core, inv[r * XS + tx]]
        core_copy(tx).start()
    for tx in columns:
        for r in range(ys):
            mine[tx, r] = tiles[core, inv[r * XS + tx]]
    for tx in columns:
        core_copy(tx).wait_recv()
        mine[tx] = mine[tx] + core_in[tx]
        for ty in lines:
            @pl.when(me != ty * XS + tx)
            def _():
                m_copy(ty * XS + tx).start()
    m_in[me] = mine[x, y]
    m_all().wait_recv()
    total = jnp.sum(m_in[...], axis=0)
    for r in range(4):
        z_out[r] = total[2 * r:2 * r + 2, :]

    def rows_of(o):
        return lax.rem(o, 2) * 2 + jnp.where(o // 2 >= groups, 1, 0)

    def other_plane(i):
        return i - jnp.where(i > z, 0, 1)

    def z_copy(i):
        to = other_plane(i)
        return pltpu.make_async_remote_copy(
            src_ref=z_out.at[rows_of(to)],
            dst_ref=z_in.at[z],
            send_sem=z_send_sem,
            recv_sem=z_recv_sem,
            device_id=(to * 2 + core, me),
            device_id_type=MESH,
        )

    def z_all():
        return pltpu.make_async_remote_copy(
            src_ref=z_in.at[1:],
            dst_ref=z_in.at[1:],
            send_sem=z_send_sem,
            recv_sem=z_recv_sem,
            device_id=(grp, me),
            device_id_type=MESH,
        )

    for i in range(1, zs):
        z_copy(i).start()
    z_in[z] = z_out[rows_of(z)]
    z_all().wait_recv()
    owned = jnp.sum(z_in[...], axis=0)
    group = lax.rem(z // 2, groups)
    out = owned[:, 0:n]
    for k in range(1, groups):
        out = jnp.where(group == k, owned[:, k * n:(k + 1) * n], out)
    out_ref[...] = out

    tile_all().wait_send()
    pltpu.make_async_copy(other, core_in, c_send_sem).wait()
    m_all().wait_send()
    z_all().wait_send()


def body(t_store, v_blocks, block_id, tile_home, task_slab):
    mems = lax.axis_size("mem")
    ys = mems // XS
    zs = lax.axis_size("grp") // 2
    nob, ot, width = t_store.shape
    tasks, n, _ = v_blocks.shape
    lanes = zs // 4 * n
    any_ref = pl.BlockSpec(memory_space=pl.ANY)
    dma = pltpu.SemaphoreType.DMA
    return pl.pallas_call(
        kernel,
        out_shape=jax.ShapeDtypeStruct((2, n), jnp.float32),
        in_specs=[any_ref] * 5,
        out_specs=pl.BlockSpec(memory_space=pltpu.VMEM),
        scratch_shapes=[
            pltpu.VMEM((nob, ot, width), jnp.bfloat16),
            pltpu.VMEM((tasks * n, width), jnp.bfloat16),
            pltpu.VMEM((mems, ot, width), jnp.bfloat16),
            pltpu.VMEM((mems, ot, width), jnp.bfloat16),
            pltpu.VMEM((nob * ot, width), jnp.bfloat16),
            pltpu.VMEM((2, tasks + 1, 8, lanes), jnp.float32),
            pltpu.VMEM((XS, ys, 8, lanes), jnp.float32),
            pltpu.VMEM((XS, ys, 8, lanes), jnp.float32),
            pltpu.VMEM((XS, ys, 8, lanes), jnp.float32),
            pltpu.VMEM((mems, 8, lanes), jnp.float32),
            pltpu.VMEM((4, 2, lanes), jnp.float32),
            pltpu.VMEM((zs, 2, lanes), jnp.float32),
            pltpu.SMEM(block_id.shape, jnp.int32),
            pltpu.SMEM(tile_home.shape, jnp.int32),
            pltpu.SMEM((tasks, 1, mems), jnp.int32),
            pltpu.SMEM((mems,), jnp.int32),
            dma((5,)),
            dma,
            dma,
            dma,
            dma((XS,)),
            dma,
            dma,
            dma,
            dma,
            pltpu.SemaphoreType.REGULAR((ys // 2,)),
            pltpu.SemaphoreType.REGULAR,
            pltpu.SemaphoreType.REGULAR,
            pltpu.SemaphoreType.REGULAR,
        ],
        compiler_params=pltpu.CompilerParams(
            collective_id=0, has_side_effects=True, vmem_limit_bytes=60 * 1024 * 1024
        ),
        name="ladder",
    )(t_store, v_blocks.reshape(tasks * n, width), block_id, tile_home, jnp.transpose(task_slab, (2, 0, 1)))


def solution(mesh):
    return jax.shard_map(
        body,
        mesh=mesh,
        in_specs=(
            P(("grp", "mem"), None, None),
            P(("grp", "mem"), None, None),
            P("grp", None),
            P("grp", None),
            P("grp", None, None),
        ),
        out_specs=P("grp", "mem"),
        check_vma=False,
    )
```

```python
import functools

import jax
import jax.numpy as jnp
from jax import lax
from jax.experimental import pallas as pl
from jax.experimental.pallas import tpu as pltpu
from jax.sharding import PartitionSpec as P

MESH = pl.DeviceIdType.MESH
XS = 4


def farthest_first(size):
    return sorted(range(size), key=lambda d: -min(d, size - d))


def kernel(
    t_hbm, v_hbm, bid_hbm, home_hbm, slab_hbm, out_ref,
    t_v, v_v, send, recv, col, tiles, mine, other, core_in, m_in, z_out, z_in,
    bid, home, slab, inv,
    in_sem, t_send_sem, t_recv_sem, c_send_sem, c_recv_sem, m_send_sem, m_recv_sem,
    z_send_sem, z_recv_sem, near_sem, above_sem, up_sem, all_sem,
):
    mems = lax.axis_size("mem")
    grps = lax.axis_size("grp")
    ys = mems // XS
    zs = grps // 2
    nob, ot = t_v.shape[0], t_v.shape[1]
    tasks = slab.shape[0]
    n = out_ref.shape[1]
    groups = zs // 4

    me = lax.axis_index("mem")
    grp = lax.axis_index("grp")
    y, x = me // XS, lax.rem(me, XS)
    z, core = grp // 2, lax.rem(grp, 2)

    at_y = [lax.rem(y + dy, ys) for dy in range(ys)]
    at_x = [lax.rem(x + dx, XS) for dx in range(XS)]
    x_order = farthest_first(XS)

    def mem_peer(dy, dx):
        return at_y[dy] * XS + at_x[dx]

    barrier = pltpu.get_barrier_semaphore()
    near = [(dy, dx) for dx in x_order for dy in (1, ys - 1, 0) if dy or dx]
    for dy, dx in near:
        pl.semaphore_signal(barrier, inc=1, device_id=(grp, mem_peer(dy, dx)), device_id_type=MESH)
    sibling = z * 2 + 1 - core
    pl.semaphore_signal(barrier, inc=1, device_id=(sibling, me), device_id_type=MESH)

    def tell(to, semaphore):
        pl.semaphore_signal(semaphore, inc=1, device_id=(to * 2 + core, me), device_id_type=MESH)

    @pl.when(z < zs - 1)
    def _():
        tell(z + 1, barrier)

    loads = [
        pltpu.make_async_copy(src, dst, in_sem.at[i])
        for i, (src, dst) in enumerate(
            ((t_hbm, t_v), (home_hbm, home), (bid_hbm, bid), (slab_hbm, slab), (v_hbm, v_v))
        )
    ]
    for load in loads[:3]:
        load.start()

    for load in loads[:3]:
        load.wait()
    for load in loads[3:]:
        load.start()

    def tile_for(p):
        q = bid[0, p]
        start = home[0, q * nob] // nob
        o = lax.rem(me - start + mems, mems)
        return lax.rem(home[0, q * nob + jnp.minimum(o, nob - 1)], nob)

    def tile_copy(dy, dx):
        slot = dy * XS + dx
        return pltpu.make_async_remote_copy(
            src_ref=send.at[slot],
            dst_ref=recv.at[slot],
            send_sem=t_send_sem,
            recv_sem=t_recv_sem,
            device_id=(grp, mem_peer(dy, dx)),
            device_id_type=MESH,
        )

    def tile_all():
        return pltpu.make_async_remote_copy(
            src_ref=send.at[1:],
            dst_ref=recv.at[1:],
            send_sem=t_send_sem,
            recv_sem=t_recv_sem,
            device_id=(grp, me),
            device_id_type=MESH,
        )

    pl.semaphore_wait(barrier, len(near) + 1 + jnp.where(z > 0, 1, 0))

    @pl.when(z > 0)
    def _():
        tell(z - 1, above_sem)

    def tell_rows(d):
        for dy in (1, ys - 1):
            pl.semaphore_signal(near_sem.at[d], inc=1, device_id=(grp, mem_peer(dy, 0)), device_id_type=MESH)

    tell_rows(1)
    half = ys // 2
    last = sorted({half, half - 1, ys - half + 1} - {1, ys - 1}, key=lambda d: -min(d, ys - d))
    plan = [near]
    plan += [[(dy, dx) for dx in x_order for dy in (d, ys - d)] for d in range(2, half - 1)]
    plan += [[(dy, dx) for dx in x_order for dy in last]]
    known = 1
    for rows in plan:
        for d in range(known + 1, max(min(dy, ys - dy) for dy, _ in rows) + 1):
            pl.semaphore_wait(near_sem.at[d - 1], 2)
            if d < half:
                tell_rows(d)
            known = d
        for dy, dx in rows:
            send[dy * XS + dx] = t_v[tile_for(mem_peer(dy, dx))]
            tile_copy(dy, dx).start()
    recv[0] = t_v[tile_for(me)]

    @pl.when(z < zs - 1)
    def _():
        pl.semaphore_wait(above_sem, 1)

    @pl.when(z > 0)
    def _():
        pl.semaphore_wait(up_sem, 1)

    @pl.when(z < zs - 1)
    def _():
        tell(z + 1, up_sem)

    @pl.when(z == zs - 1)
    def _():
        for to in range(zs - 1):
            tell(to, all_sem)

    def locate(p, c):
        at = jnp.int32(tasks)
        for b in range(tasks):
            at = jnp.where(slab[b, 0, me] == p, b, at)
        inv[p] = at
        return c

    loads[3].wait()
    lax.fori_loop(0, mems, locate, 0)
    tiles[...] = jnp.zeros_like(tiles)
    loads[4].wait()

    @pl.when(z < zs - 1)
    def _():
        pl.semaphore_wait(all_sem, 1)

    tile_all().wait_recv()

    first = home[0, bid[0, me] * nob] // nob
    for o in range(nob):
        src = lax.rem(first + o, mems)
        dy = lax.rem(y - src // XS + ys, ys)
        dx = lax.rem(x - lax.rem(src, XS) + XS, XS)
        t = dy * XS + dx
        col[o * ot:(o + 1) * ot, :] = recv[t]

    result = lax.dot_general(
        col[...], v_v[...], (((1,), (1,)), ((), ())), preferred_element_type=jnp.float32
    )

    row = lax.broadcasted_iota(jnp.int32, (8, n), 0)
    upper = lax.rem(row // 2, 2) == 1
    for b in range(tasks):
        for c in range(2):
            parts = []
            for k in range(groups):
                lo = result[k * 8:(k + 1) * 8, b * n:(b + 1) * n]
                hi = result[(k + groups) * 8:(k + groups + 1) * 8, b * n:(b + 1) * n]
                if c == 0:
                    parts.append(jnp.where(upper, pltpu.roll(hi, 2, 0), lo))
                else:
                    parts.append(jnp.where(upper, hi, pltpu.roll(lo, 6, 0)))
            tiles[c, b] = jnp.concatenate(parts, axis=1) if groups > 1 else parts[0]

    def core_copy(tx):
        return pltpu.make_async_remote_copy(
            src_ref=other.at[tx],
            dst_ref=core_in.at[tx],
            send_sem=c_send_sem,
            recv_sem=c_recv_sem.at[tx],
            device_id=(sibling, me),
            device_id_type=MESH,
        )

    def m_copy(p):
        return pltpu.make_async_remote_copy(
            src_ref=mine.at[p % XS, p // XS],
            dst_ref=m_in.at[me],
            send_sem=m_send_sem,
            recv_sem=m_recv_sem,
            device_id=(grp, p),
            device_id_type=MESH,
        )

    def m_all():
        return pltpu.make_async_remote_copy(
            src_ref=m_in.at[1:],
            dst_ref=m_in.at[1:],
            send_sem=m_send_sem,
            recv_sem=m_recv_sem,
            device_id=(grp, me),
            device_id_type=MESH,
        )

    columns, lines = farthest_first(XS)[::-1], farthest_first(ys)[::-1]
    for tx in columns:
        for r in range(ys):
            other[tx, r] = tiles[1 - core, inv[r * XS + tx]]
        core_copy(tx).start()
    for tx in columns:
        for r in range(ys):
            mine[tx, r] = tiles[core, inv[r * XS + tx]]
    for tx in columns:
        core_copy(tx).wait_recv()
        mine[tx] = mine[tx] + core_in[tx]
        for ty in lines:
            @pl.when(me != ty * XS + tx)
            def _():
                m_copy(ty * XS + tx).start()
    m_in[me] = mine[x, y]
    m_all().wait_recv()
    total = jnp.sum(m_in[...], axis=0)
    for r in range(4):
        z_out[r] = total[2 * r:2 * r + 2, :]

    def rows_of(o):
        return lax.rem(o, 2) * 2 + jnp.where(o // 2 >= groups, 1, 0)

    def other_plane(i):
        return i - jnp.where(i > z, 0, 1)

    def z_copy(i):
        to = other_plane(i)
        return pltpu.make_async_remote_copy(
            src_ref=z_out.at[rows_of(to)],
            dst_ref=z_in.at[z],
            send_sem=z_send_sem,
            recv_sem=z_recv_sem,
            device_id=(to * 2 + core, me),
            device_id_type=MESH,
        )

    def z_all():
        return pltpu.make_async_remote_copy(
            src_ref=z_in.at[1:],
            dst_ref=z_in.at[1:],
            send_sem=z_send_sem,
            recv_sem=z_recv_sem,
            device_id=(grp, me),
            device_id_type=MESH,
        )

    for i in range(1, zs):
        z_copy(i).start()
    z_in[z] = z_out[rows_of(z)]
    tile_all().wait_send()
    pltpu.make_async_copy(other, core_in, c_send_sem).wait()
    m_all().wait_send()
    z_all().wait_recv()
    owned = jnp.sum(z_in[...], axis=0)
    group = lax.rem(z // 2, groups)
    out = owned[:, 0:n]
    for k in range(1, groups):
        out = jnp.where(group == k, owned[:, k * n:(k + 1) * n], out)
    out_ref[...] = out

    z_all().wait_send()


def body(t_store, v_blocks, block_id, tile_home, task_slab):
    mems = lax.axis_size("mem")
    ys = mems // XS
    zs = lax.axis_size("grp") // 2
    nob, ot, width = t_store.shape
    tasks, n, _ = v_blocks.shape
    lanes = zs // 4 * n
    any_ref = pl.BlockSpec(memory_space=pl.ANY)
    dma = pltpu.SemaphoreType.DMA
    return pl.pallas_call(
        kernel,
        out_shape=jax.ShapeDtypeStruct((2, n), jnp.float32),
        in_specs=[any_ref] * 5,
        out_specs=pl.BlockSpec(memory_space=pltpu.VMEM),
        scratch_shapes=[
            pltpu.VMEM((nob, ot, width), jnp.bfloat16),
            pltpu.VMEM((tasks * n, width), jnp.bfloat16),
            pltpu.VMEM((mems, ot, width), jnp.bfloat16),
            pltpu.VMEM((mems, ot, width), jnp.bfloat16),
            pltpu.VMEM((nob * ot, width), jnp.bfloat16),
            pltpu.VMEM((2, tasks + 1, 8, lanes), jnp.float32),
            pltpu.VMEM((XS, ys, 8, lanes), jnp.float32),
            pltpu.VMEM((XS, ys, 8, lanes), jnp.float32),
            pltpu.VMEM((XS, ys, 8, lanes), jnp.float32),
            pltpu.VMEM((mems, 8, lanes), jnp.float32),
            pltpu.VMEM((4, 2, lanes), jnp.float32),
            pltpu.VMEM((zs, 2, lanes), jnp.float32),
            pltpu.SMEM(block_id.shape, jnp.int32),
            pltpu.SMEM(tile_home.shape, jnp.int32),
            pltpu.SMEM((tasks, 1, mems), jnp.int32),
            pltpu.SMEM((mems,), jnp.int32),
            dma((5,)),
            dma,
            dma,
            dma,
            dma((XS,)),
            dma,
            dma,
            dma,
            dma,
            pltpu.SemaphoreType.REGULAR((ys // 2,)),
            pltpu.SemaphoreType.REGULAR,
            pltpu.SemaphoreType.REGULAR,
            pltpu.SemaphoreType.REGULAR,
        ],
        compiler_params=pltpu.CompilerParams(
            collective_id=0, has_side_effects=True, vmem_limit_bytes=60 * 1024 * 1024
        ),
        name="ladder",
    )(t_store, v_blocks.reshape(tasks * n, width), block_id, tile_home, jnp.transpose(task_slab, (2, 0, 1)))


def solution(mesh):
    return jax.shard_map(
        body,
        mesh=mesh,
        in_specs=(
            P(("grp", "mem"), None, None),
            P(("grp", "mem"), None, None),
            P("grp", None),
            P("grp", None),
            P("grp", None, None),
        ),
        out_specs=P("grp", "mem"),
        check_vma=False,
    )
```
